32 devices in a mesh: atoms: 8 (over y, x, core), chan: 4 (over z).
Axes of the slice: x: 2, y: 2, z: 4, core: 2. Of those that a mesh axis runs over, the one named last changes fastest.
Arguments:
- features: bfloat16 [16384, 512], P('atoms', 'chan'), may hold values from -6 to 6
- positions: int32 [3, 16384], P(None, 'atoms'), may hold values from 0 to 4095
- wavevectors: int32 [3, 2048], replicated, may hold values from -8 to 8
- radial_weight: float32 [16, 512], P(None, 'chan'), may hold values from -6 to 6
- weight_in: bfloat16 [512, 1024], replicated, may hold values from -0.25 to 0.25
- weight_out: bfloat16 [1024, 512], replicated, may hold values from -0.1875 to 0.1875
- cotangent: bfloat16 [16384, 512], P('atoms', 'chan'), may hold values from -6 to 6
Outputs:
- output: bfloat16 [16384, 512], P('atoms', 'chan')
- feature_grad: float32 [16384, 512], P('atoms', 'chan')
The draws below stay inside these ranges and needn't reach their ends.
All inputs are finite; a program needn't handle non-finite values.
Results may differ from the reference program's by a relative error of at most 0.0057.
Values may be sent and summed in bfloat16 or wider, within the bound.
A program may use at most 128 MiB of HBM per device.

```python
import math
import jax
import jax.numpy as jnp
from jax import lax

C = 512
KVEC = 2048
HIDDEN_SIZE = 1024
NB = 16
KMAX = 8
GRID = 4096
ATOMS_DEV = 2048
ATOMS = 16384


def place_ends(result, own_key, smallest, largest):
    place = [jax.random.randint(jax.random.fold_in(own_key, axis), (), 0, length) for axis, length in enumerate(result.shape)]
    main_axis = result.shape.index(max(result.shape))
    next_to = place[:main_axis] + [(place[main_axis] + 1) % result.shape[main_axis]] + place[main_axis + 1:]
    return result.at[tuple(place)].set(smallest).at[tuple(next_to)].set(largest)


def level_of(stream_key, extent, cuts, low, high):
    level = 1.0
    for dim, shards_of in cuts:
        draws = jax.random.uniform(jax.random.fold_in(jax.random.fold_in(stream_key, 6), dim), (shards_of,), jnp.float32, low / len(cuts), high / len(cuts))
        level = level * jnp.repeat(jnp.exp(draws), extent[dim] // shards_of).reshape((-1,) + (1,) * (len(extent) - 1 - dim))
    return level


def normal_values(key, extent, scale, bound, pieces=(), kind=jnp.bfloat16):
    level = level_of(key, extent, pieces, -0.22, 0.18) if pieces else 1.0
    drawn = jax.random.normal(key, extent, jnp.float32) * scale * level
    return jnp.minimum(jnp.maximum(drawn, -bound), bound).astype(kind)


def setup_inputs(seed: int = 0) -> dict:
    arg_keys = jax.random.split(jax.random.key(seed), 8)
    return {
        "features": normal_values(arg_keys[0], (ATOMS, C), 1.0, 6.0, ((0, 8), (1, 4))),
        "positions": place_ends(jax.random.randint(arg_keys[1], (3, ATOMS), 0, GRID), jax.random.fold_in(arg_keys[1], 1), 0, GRID - 1).astype(jnp.int32),
        "wavevectors": place_ends(jax.random.randint(arg_keys[2], (3, KVEC), -KMAX, KMAX + 1), jax.random.fold_in(arg_keys[2], 1), -KMAX, KMAX).astype(jnp.int32),
        "radial_weight": normal_values(arg_keys[3], (NB, C), 1.0, 6.0, ((1, 4),), jnp.float32),
        "weight_in": normal_values(arg_keys[4], (C, HIDDEN_SIZE), C ** -0.5, 0.25),
        "weight_out": normal_values(arg_keys[5], (HIDDEN_SIZE, C), HIDDEN_SIZE ** -0.5, 0.1875),
        "cotangent": normal_values(arg_keys[6], (ATOMS, C), 1.0, 6.0, ((0, 8), (1, 4))),
    }


def phase_rows(wavevectors, places):
    product = wavevectors[0][:, None] * places[0][None, :]
    product = product + wavevectors[1][:, None] * places[1][None, :]
    product = product + wavevectors[2][:, None] * places[2][None, :]
    remain = jnp.mod(product, GRID)
    angles = remain.astype(jnp.float32) * (2.0 * math.pi / GRID)
    return jnp.concatenate([jnp.cos(angles), jnp.sin(angles)], 0).astype(jnp.bfloat16)

def radial_filter(wavevectors, radial_weight, atom_count):
    lengths = jnp.sqrt(lax.optimization_barrier(jnp.sum((wavevectors * wavevectors).astype(jnp.float32), 0)))
    spacing = KMAX * math.sqrt(3.0) / (NB - 1)
    centers = jnp.arange(NB).astype(jnp.float32) * spacing
    basis = jnp.exp(-0.5 * ((lengths[:, None] - centers[None, :]) / spacing) ** 2)
    filt = jnp.dot(basis, radial_weight, precision=lax.Precision.HIGHEST, preferred_element_type=jnp.float32)
    filt = filt * (2.0 * KVEC * atom_count) ** (-0.5)
    return jnp.concatenate([filt, filt], 0)

def reference(features, positions, wavevectors, radial_weight, weight_in, weight_out, cotangent):
    blocks = ATOMS // ATOMS_DEV
    place_blocks = positions.reshape(3, blocks, ATOMS_DEV).transpose(1, 0, 2)
    filt2 = radial_filter(wavevectors, radial_weight, ATOMS)

    def ewald(field):
        field_blocks = field.reshape(blocks, ATOMS_DEV, C)

        def accumulate(totals, item):
            places, block = item
            return (totals + jnp.dot(phase_rows(wavevectors, places), block, preferred_element_type=jnp.float32), None)
        totals, unused = lax.scan(accumulate, jnp.zeros((2 * KVEC, C), jnp.float32), (place_blocks, field_blocks))
        shaped = (filt2 * totals).astype(jnp.bfloat16)

        def project(places):
            return lax.dot_general(phase_rows(wavevectors, places), shaped, (((0,), (0,)), ((), ())), preferred_element_type=jnp.float32)
        return lax.map(project, place_blocks).reshape(ATOMS, C)
    message = ewald(features).astype(jnp.bfloat16)
    message_f = message.astype(jnp.float32)
    scale = jnp.sqrt(lax.optimization_barrier(jnp.mean(message_f * message_f, -1, keepdims=True)) + 1e-06)
    unit = message_f / scale
    normed = unit.astype(jnp.bfloat16)
    pre = jnp.dot(normed, weight_in, preferred_element_type=jnp.float32)
    hidden = jax.nn.silu(pre).astype(jnp.bfloat16)
    update = jnp.dot(hidden, weight_out, preferred_element_type=jnp.float32).astype(jnp.bfloat16)
    output = (features.astype(jnp.float32) + update.astype(jnp.float32)).astype(jnp.bfloat16)
    g_hidden = lax.dot_general(cotangent, weight_out, (((1,), (1,)), ((), ())), preferred_element_type=jnp.float32)
    sigmoid_pre = jax.nn.sigmoid(pre)
    g_pre = (g_hidden * sigmoid_pre * (1.0 + pre * (1.0 - sigmoid_pre))).astype(jnp.bfloat16)
    g_normed = lax.dot_general(g_pre, weight_in, (((1,), (1,)), ((), ())), preferred_element_type=jnp.float32)
    g_message = ((g_normed - unit * lax.optimization_barrier(jnp.mean(g_normed * unit, -1, keepdims=True))) / scale).astype(jnp.bfloat16)
    feature_grad = cotangent.astype(jnp.float32) + ewald(g_message)
    return (output, feature_grad)
```

```python
import functools
import math

import jax
import jax.numpy as jnp
import numpy as np
from jax import lax
from jax.experimental import pallas as pl
from jax.experimental.pallas import tpu as pltpu
from jax.sharding import PartitionSpec as P

NB = 16
KMAX = 8
GRID = 4096
MESH = pl.DeviceIdType.MESH
BLOCK = 128


def fit_even(fn, degree):
    cheb = np.polynomial.chebyshev.Chebyshev.interpolate(
        lambda u: fn(np.sqrt(u)), degree, domain=[0.0, 0.25]
    )
    return [float(v) for v in cheb.convert(kind=np.polynomial.Polynomial, domain=[-1, 1], window=[-1, 1]).coef]


def sin_over(f):
    return math.sqrt(2.0) * math.pi * np.sinc(f)


def cos_half(f):
    return math.sqrt(2.0) * np.cos(math.pi * f)


SIN_COEF = fit_even(sin_over, 3)
COS_COEF = fit_even(cos_half, 3)


def horner(coef, u):
    total = coef[-1] * u + coef[-2]
    for c in coef[-3::-1]:
        total = total * u + c
    return total


def ewald_kernel(first, n, chunks, *refs):
    if first:
        (wave_ref, place_ref, x_ref, filt_ref, out_ref, phases_out,
         ph, part, rs_src, rs_dst, ag, acc, local_sem, rs_send, rs_recv, ag_send, ag_recv) = refs
    else:
        (phases_in, x_ref, filt_ref, cot_ref, out_ref,
         ph, part, rs_src, rs_dst, ag, acc, local_sem, rs_send, rs_recv, ag_send, ag_recv) = refs
    me = lax.axis_index("atoms")
    atoms = x_ref.shape[0]
    rows = n * BLOCK
    waves = rows // 2

    def local_copy(j):
        span = pl.ds(j * rows, rows)
        if first:
            return pltpu.make_async_copy(ph.at[span], phases_out.at[span], local_sem.at[j])
        return pltpu.make_async_copy(phases_in.at[span], ph.at[span], local_sem.at[j])

    if not first:
        for j in range(chunks):
            local_copy(j).start()

    barrier = pltpu.get_barrier_semaphore()

    def greet(step, carry):
        pl.semaphore_signal(
            barrier, inc=1, device_id={"atoms": lax.rem(me + step, n)}, device_id_type=MESH
        )
        return carry

    lax.fori_loop(1, n, greet, 0)

    def rs_copy(j, here, there):
        return pltpu.make_async_remote_copy(
            src_ref=rs_src.at[j, there],
            dst_ref=rs_dst.at[j, here],
            send_sem=rs_send.at[j, there],
            recv_sem=rs_recv.at[j, here],
            device_id={"atoms": there},
            device_id_type=MESH,
        )

    def ag_copy(j, owner, there):
        return pltpu.make_async_remote_copy(
            src_ref=ag.at[j, owner],
            dst_ref=ag.at[j, owner],
            send_sem=ag_send.at[j, there],
            recv_sem=ag_recv.at[j, owner],
            device_id={"atoms": there},
            device_id_type=MESH,
        )

    def peers(fn):
        def body(step, carry):
            fn(lax.rem(me + step, n))
            return carry

        lax.fori_loop(1, n, body, 0)

    tile = min(256, atoms)

    def generate(j):
        top = j * rows

        def body(a, carry):
            cols = pl.ds(pl.multiple_of(a * tile, tile), tile)
            turns = jnp.dot(
                wave_ref[pl.ds(j * waves, waves), :], place_ref[:, cols],
                preferred_element_type=jnp.float32,
            )
            f = turns - jnp.round(turns)
            u = f * f
            s = f * horner(SIN_COEF, u)
            c = horner(COS_COEF, u)
            ph[pl.ds(top, waves), cols] = (1.0 - s * s).astype(jnp.bfloat16)
            ph[pl.ds(top + waves, waves), cols] = (s * c).astype(jnp.bfloat16)
            return carry

        lax.fori_loop(0, atoms // tile, body, 0)

    group = min(4, n)

    def project(j):
        def body(i, carry):
            span = pl.ds(pl.multiple_of(j * rows + i * (group * BLOCK), group * BLOCK), group * BLOCK)
            value = jnp.dot(ph[span, :], x_ref[...], preferred_element_type=jnp.float32)
            value = value.reshape(group, BLOCK, value.shape[-1])
            slots = pl.ds(i * group, group)
            part[j, slots] = value
            rs_src[j, slots] = value.astype(jnp.bfloat16)
            return carry

        lax.fori_loop(0, n // group, body, 0)

    def reduce(j):
        part_own = part[j, me]

        def body(step, total):
            peer = lax.rem(me + step, n)
            rs_copy(j, peer, me).wait_recv()
            return total + rs_dst[j, peer].astype(jnp.float32)

        total = lax.fori_loop(1, n, body, part_own)
        shaped = filt_ref[pl.ds(j * BLOCK, BLOCK), :] * total
        ag[j, me] = shaped.T.astype(jnp.bfloat16)
        peers(lambda peer: ag_copy(j, me, peer).start())

    wide = min(512, atoms)

    def back(j):
        peers(lambda peer: ag_copy(j, peer, me).wait_recv())
        lhs = jnp.concatenate([ag[j, d] for d in range(n)], axis=1)

        def body(a, carry):
            cols = pl.ds(pl.multiple_of(a * wide, wide), wide)
            value = jnp.dot(lhs, ph[pl.ds(j * rows, rows), cols], preferred_element_type=jnp.float32)
            if j > 0:
                value = value + acc[:, cols]
            if j < chunks - 1:
                acc[:, cols] = value
            elif first:
                out_ref[cols, :] = value.T.astype(jnp.bfloat16)
            else:
                out_ref[cols, :] = cot_ref[cols, :].astype(jnp.float32) + value.T
            return carry

        lax.fori_loop(0, atoms // wide, body, 0)

    for j in range(chunks + 2):
        if j < chunks:
            if first:
                generate(j)
                local_copy(j).start()
            else:
                local_copy(j).wait()
            project(j)
            if j == 0:
                pl.semaphore_wait(barrier, n - 1)
            peers(lambda peer: rs_copy(j, me, peer).start())
        if 1 <= j <= chunks:
            reduce(j - 1)
        if j >= 2:
            back(j - 2)

    for j in range(chunks):
        if first:
            local_copy(j).wait()
        peers(lambda peer: rs_copy(j, me, peer).wait_send())
        peers(lambda peer: ag_copy(j, me, peer).wait_send())


def ewald(first, n, total_rows, *operands):
    field = operands[2] if first else operands[1]
    atoms, channels = field.shape
    chunks = total_rows // (n * BLOCK)
    vmem = pl.BlockSpec(memory_space=pltpu.VMEM)
    anywhere = pl.BlockSpec(memory_space=pl.ANY)
    if first:
        in_specs = [vmem] * 4
        out_shape = (
            jax.ShapeDtypeStruct((atoms, channels), jnp.bfloat16),
            jax.ShapeDtypeStruct((total_rows, atoms), jnp.bfloat16),
        )
        out_specs = (vmem, anywhere)
    else:
        in_specs = [anywhere] + [vmem] * 3
        out_shape = jax.ShapeDtypeStruct((atoms, channels), jnp.float32)
        out_specs = vmem
    block = (chunks, n, BLOCK, channels)
    sems = pltpu.SemaphoreType.DMA((chunks, n))
    return pl.pallas_call(
        functools.partial(ewald_kernel, first, n, chunks),
        out_shape=out_shape,
        in_specs=in_specs,
        out_specs=out_specs,
        scratch_shapes=[
            pltpu.VMEM((total_rows, atoms), jnp.bfloat16),
            pltpu.VMEM(block, jnp.float32),
            pltpu.VMEM(block, jnp.bfloat16),
            pltpu.VMEM(block, jnp.bfloat16),
            pltpu.VMEM((chunks, n, channels, BLOCK), jnp.bfloat16),
            pltpu.VMEM((channels, atoms), jnp.float32),
            pltpu.SemaphoreType.DMA((chunks,)),
            sems, sems, sems, sems,
        ],
        compiler_params=pltpu.CompilerParams(
            collective_id=0 if first else 1, has_side_effects=True, vmem_limit_bytes=44 * 2**20
        ),
        name="ewald_first" if first else "ewald_second",
    )(*operands)


def own_filter(wavevectors, radial_weight, atom_count, n, me):
    kvec = wavevectors.shape[1]
    waves = n * BLOCK // 2
    chunked = wavevectors.reshape(3, kvec // waves, n // 2, BLOCK)
    own = lax.dynamic_index_in_dim(chunked, lax.rem(me, n // 2), 2, keepdims=False).reshape(3, -1)
    lengths = jnp.sqrt(jnp.sum((own * own).astype(jnp.float32), 0))
    spacing = KMAX * math.sqrt(3.0) / (NB - 1)
    centers = jnp.arange(NB).astype(jnp.float32) * spacing
    basis = jnp.exp(-0.5 * ((lengths[:, None] - centers[None, :]) / spacing) ** 2)
    filt = jnp.dot(
        basis, radial_weight, precision=lax.Precision.HIGHEST, preferred_element_type=jnp.float32
    )
    return filt * (2.0 * kvec * atom_count) ** (-0.5)


def shards(features, positions, wavevectors, radial_weight, weight_in, weight_out, cotangent):
    local_atoms = features.shape[0]
    n = lax.axis_size("atoms")
    atom_count = local_atoms * n
    total_rows = 2 * wavevectors.shape[1]
    filt = own_filter(wavevectors, radial_weight, atom_count, n, lax.axis_index("atoms"))

    wave = wavevectors.T.astype(jnp.float32)
    wave = jnp.concatenate([wave * (64.0 / GRID), wave * (1.0 / GRID)], 1)
    wave = jnp.pad(wave, ((0, 0), (0, 10))).astype(jnp.bfloat16)
    place = jnp.concatenate([positions // 64, positions % 64], 0)
    place = jnp.pad(place, ((0, 10), (0, 0))).astype(jnp.bfloat16)

    message, phases = ewald(True, n, total_rows, wave, place, features, filt)
    row_message, row_cotangent = (
        lax.all_to_all(message, "chan", split_axis=0, concat_axis=1, tiled=True),
        lax.all_to_all(cotangent, "chan", split_axis=0, concat_axis=1, tiled=True),
    )
    message_f = row_message.astype(jnp.float32)
    scale = jnp.sqrt(jnp.mean(message_f * message_f, -1, keepdims=True) + 1e-06)
    unit = message_f / scale
    normed = unit.astype(jnp.bfloat16)
    pre = jnp.dot(normed, weight_in, preferred_element_type=jnp.float32)
    hidden = jax.nn.silu(pre).astype(jnp.bfloat16)
    update = jnp.dot(hidden, weight_out, preferred_element_type=jnp.float32).astype(jnp.bfloat16)
    g_hidden = lax.dot_general(
        row_cotangent, weight_out, (((1,), (1,)), ((), ())), preferred_element_type=jnp.float32
    )
    sigmoid_pre = jax.nn.sigmoid(pre)
    g_pre = (g_hidden * sigmoid_pre * (1.0 + pre * (1.0 - sigmoid_pre))).astype(jnp.bfloat16)
    g_normed = lax.dot_general(
        g_pre, weight_in, (((1,), (1,)), ((), ())), preferred_element_type=jnp.float32
    )
    g_message = ((g_normed - unit * jnp.mean(g_normed * unit, -1, keepdims=True)) / scale).astype(
        jnp.bfloat16
    )
    chan_update, chan_gradient = (
        lax.all_to_all(update, "chan", split_axis=1, concat_axis=0, tiled=True),
        lax.all_to_all(g_message, "chan", split_axis=1, concat_axis=0, tiled=True),
    )
    output = (features.astype(jnp.float32) + chan_update.astype(jnp.float32)).astype(jnp.bfloat16)
    feature_grad = ewald(False, n, total_rows, phases, chan_gradient, filt, cotangent)
    return (output, feature_grad)


def solution(mesh):
    placed = (
        P("atoms", "chan"),
        P(None, "atoms"),
        P(),
        P(None, "chan"),
        P(),
        P(),
        P("atoms", "chan"),
    )
    return jax.shard_map(
        shards,
        mesh=mesh,
        in_specs=placed,
        out_specs=(P("atoms", "chan"), P("atoms", "chan")),
        check_vma=False,
    )
```

```python
import functools
import math

import jax
import jax.numpy as jnp
import numpy as np
from jax import lax
from jax.experimental import pallas as pl
from jax.experimental.pallas import tpu as pltpu
from jax.sharding import PartitionSpec as P

NB = 16
KMAX = 8
GRID = 4096
MESH = pl.DeviceIdType.MESH
BLOCK = 128


def fit_even(fn, degree):
    cheb = np.polynomial.chebyshev.Chebyshev.interpolate(
        lambda u: fn(np.sqrt(u)), degree, domain=[0.0, 0.25]
    )
    return [float(v) for v in cheb.convert(kind=np.polynomial.Polynomial, domain=[-1, 1], window=[-1, 1]).coef]


def sin_over(f):
    return math.sqrt(2.0) * math.pi * np.sinc(f)


def cos_half(f):
    return math.sqrt(2.0) * np.cos(math.pi * f)


SIN_COEF = fit_even(sin_over, 3)
COS_COEF = fit_even(cos_half, 3)


def horner(coef, u):
    total = coef[-1] * u + coef[-2]
    for c in coef[-3::-1]:
        total = total * u + c
    return total


def layer_kernel(n, nc, chunks, *refs):
    (waves_in, place_in, x_ref, filt_ref, w_in, w_out, cot_ref, out_ref, grad_ref,
     wave_ref, place_ref, ph, part, rs_src, rs_dst, ag, acc,
     cot_rx, msg_tx, msg_rx, upd_tx, upd_rx, grd_tx, grd_rx,
     rs_send, rs_recv, ag_send, ag_recv, cot_send, cot_recv,
     msg_send, msg_recv, upd_send, upd_recv, grd_send, grd_recv) = refs
    me = lax.axis_index("atoms")
    mc = lax.axis_index("chan")
    atoms, channels = x_ref.shape
    rows = n * BLOCK
    waves = rows // 2
    own = atoms // nc
    sub = min(BLOCK, own)
    subs = own // sub
    f32, bf16 = jnp.float32, jnp.bfloat16

    def peers(fn):
        def body(step, carry):
            fn(lax.rem(me + step, n))
            return carry

        lax.fori_loop(1, n, body, 0)

    def chan_peers(fn):
        def body(step, carry):
            fn(lax.rem(mc + step, nc))
            return carry

        lax.fori_loop(1, nc, body, 0)

    barrier = pltpu.get_barrier_semaphore()
    peers(lambda peer: pl.semaphore_signal(
        barrier, inc=1, device_id={"atoms": peer}, device_id_type=MESH))
    chan_peers(lambda peer: pl.semaphore_signal(
        barrier, inc=1, device_id={"chan": peer}, device_id_type=MESH))

    def rs_copy(j, here, there):
        return pltpu.make_async_remote_copy(
            src_ref=rs_src.at[j, there],
            dst_ref=rs_dst.at[j, here],
            send_sem=rs_send.at[j, there],
            recv_sem=rs_recv.at[j, here],
            device_id={"atoms": there},
            device_id_type=MESH,
        )

    def ag_copy(j, owner, there):
        return pltpu.make_async_remote_copy(
            src_ref=ag.at[j, owner],
            dst_ref=ag.at[j, owner],
            send_sem=ag_send.at[j, there],
            recv_sem=ag_recv.at[j, owner],
            device_id={"atoms": there},
            device_id_type=MESH,
        )

    def cot_copy(here, there):
        return pltpu.make_async_remote_copy(
            src_ref=cot_ref.at[pl.ds(pl.multiple_of(there * own, own), own)],
            dst_ref=cot_rx.at[here],
            send_sem=cot_send.at[there],
            recv_sem=cot_recv.at[here],
            device_id={"chan": there},
            device_id_type=MESH,
        )

    def sub_copy(src, dst, send, recv, t, here, there):
        span = pl.ds(t * sub, sub)
        return pltpu.make_async_remote_copy(
            src_ref=src.at[there, span],
            dst_ref=dst.at[here, span],
            send_sem=send.at[t, there],
            recv_sem=recv.at[t, here],
            device_id={"chan": there},
            device_id_type=MESH,
        )

    msg_copy = functools.partial(sub_copy, msg_tx, msg_rx, msg_send, msg_recv)
    upd_copy = functools.partial(sub_copy, upd_tx, upd_rx, upd_send, upd_recv)
    grd_copy = functools.partial(sub_copy, grd_tx, grd_rx, grd_send, grd_recv)

    k = waves_in[...].astype(f32)
    wave_ref[...] = jnp.concatenate(
        [k * (64.0 / GRID), k * (1.0 / GRID), jnp.zeros((10, k.shape[1]), f32)], 0
    ).astype(bf16)
    r = place_in[...]
    high = lax.shift_right_logical(r, 6)
    place_ref[...] = jnp.concatenate(
        [high.astype(f32), (r - high * 64).astype(f32), jnp.zeros((10, r.shape[1]), f32)], 0
    ).astype(bf16)

    tile = min(256, atoms)

    def generate(j):
        top = j * rows

        def body(a, carry):
            cols = pl.ds(pl.multiple_of(a * tile, tile), tile)
            turns = lax.dot_general(
                wave_ref[:, pl.ds(j * waves, waves)], place_ref[:, cols],
                (((0,), (0,)), ((), ())), preferred_element_type=f32,
            )
            f = turns - jnp.round(turns)
            u = f * f
            s = f * horner(SIN_COEF, u)
            c = horner(COS_COEF, u)
            ph[pl.ds(top, waves), cols] = (1.0 - s * s).astype(bf16)
            ph[pl.ds(top + waves, waves), cols] = (s * c).astype(bf16)
            return carry

        lax.fori_loop(0, atoms // tile, body, 0)

    group = min(4, n)

    def project(j, field):
        def body(i, carry):
            span = pl.ds(pl.multiple_of(j * rows + i * (group * BLOCK), group * BLOCK), group * BLOCK)
            value = jnp.dot(ph[span, :], field(), preferred_element_type=f32)
            value = value.reshape(group, BLOCK, value.shape[-1])
            slots = pl.ds(i * group, group)
            part[j, slots] = value
            rs_src[j, slots] = value.astype(bf16)
            return carry

        lax.fori_loop(0, n // group, body, 0)

    def reduce(j):
        part_own = part[j, me]

        def body(step, total):
            peer = lax.rem(me + step, n)
            rs_copy(j, peer, me).wait_recv()
            return total + rs_dst[j, peer].astype(f32)

        total = lax.fori_loop(1, n, body, part_own)
        shaped = filt_ref[pl.ds(j * BLOCK, BLOCK), :] * total
        ag[j, me] = shaped.T.astype(bf16)
        peers(lambda peer: ag_copy(j, me, peer).start())

    def back(j, emit):
        peers(lambda peer: ag_copy(j, peer, me).wait_recv())
        lhs = jnp.concatenate([ag[j, d] for d in range(n)], axis=1)

        def body(a, carry):
            cols = pl.ds(pl.multiple_of(a * own, own), own)
            value = jnp.dot(lhs, ph[pl.ds(j * rows, rows), cols], preferred_element_type=f32)
            if j > 0:
                value = value + acc[:, cols]
            if j < chunks - 1:
                acc[:, cols] = value
            else:
                emit(a, value.T)
            return carry

        lax.fori_loop(0, nc, body, 0)

    def ewald(first, field, emit):
        for j in range(chunks + 2):
            if j < chunks:
                if first:
                    generate(j)
                project(j, field)
                if first and j == 0:
                    pl.semaphore_wait(barrier, n - 1 + nc - 1)
                    chan_peers(lambda peer: cot_copy(mc, peer).start())
                peers(lambda peer: rs_copy(j, me, peer).start())
            if 1 <= j <= chunks:
                reduce(j - 1)
            if j >= 2:
                back(j - 2, emit)
        for j in range(chunks):
            peers(lambda peer: rs_copy(j, me, peer).wait_send())
            peers(lambda peer: ag_copy(j, me, peer).wait_send())

    def emit_message(a, value):
        msg_tx[a] = value.astype(bf16)

    ewald(True, lambda: x_ref[...], emit_message)

    for t in range(subs):
        chan_peers(lambda peer: msg_copy(t, mc, peer).start())
    msg_rx[mc] = msg_tx[mc]
    cot_rx[mc] = cot_ref[pl.ds(pl.multiple_of(mc * own, own), own), :]
    chan_peers(lambda peer: cot_copy(peer, mc).wait_recv())

    for t in range(subs):
        span = pl.ds(t * sub, sub)
        chan_peers(lambda peer: msg_copy(t, peer, mc).wait_recv())
        message = jnp.concatenate([msg_rx[c, span, :] for c in range(nc)], 1).astype(f32)
        inverse = 1.0 / jnp.sqrt(jnp.mean(message * message, -1, keepdims=True) + 1e-06)
        unit = message * inverse
        pre = jnp.dot(unit.astype(bf16), w_in[...], preferred_element_type=f32)
        gate = jax.nn.sigmoid(pre)
        update = jnp.dot((pre * gate).astype(bf16), w_out[...], preferred_element_type=f32)
        cot = jnp.concatenate([cot_rx[c, span, :] for c in range(nc)], 1)
        g_hidden = lax.dot_general(
            cot, w_out[...], (((1,), (1,)), ((), ())), preferred_element_type=f32
        )
        g_pre = (g_hidden * gate * (1.0 + pre * (1.0 - gate))).astype(bf16)
        g_normed = lax.dot_general(
            g_pre, w_in[...], (((1,), (1,)), ((), ())), preferred_element_type=f32
        )
        g_message = (
            (g_normed - unit * jnp.mean(g_normed * unit, -1, keepdims=True)) * inverse
        ).astype(bf16)
        update = update.astype(bf16)
        for c in range(nc):
            grd_tx[c, span, :] = g_message[:, c * channels:(c + 1) * channels]
            upd_tx[c, span, :] = update[:, c * channels:(c + 1) * channels]
        chan_peers(lambda peer: grd_copy(t, mc, peer).start())

    for t in range(subs):
        chan_peers(lambda peer: upd_copy(t, mc, peer).start())
    grd_rx[mc] = grd_tx[mc]
    upd_rx[mc] = upd_tx[mc]
    for t in range(subs):
        chan_peers(lambda peer: grd_copy(t, peer, mc).wait_recv())

    def emit_grad(a, value):
        span = pl.ds(pl.multiple_of(a * own, own), own)
        grad_ref[span, :] = cot_ref[span, :].astype(f32) + value

    ewald(False, lambda: grd_rx[...].reshape(atoms, channels), emit_grad)

    for t in range(subs):
        chan_peers(lambda peer: upd_copy(t, peer, mc).wait_recv())

    def add_update(c, carry):
        span = pl.ds(pl.multiple_of(c * own, own), own)
        out_ref[span, :] = (x_ref[span, :].astype(f32) + upd_rx[c].astype(f32)).astype(bf16)
        return carry

    lax.fori_loop(0, nc, add_update, 0)
    chan_peers(lambda peer: cot_copy(mc, peer).wait_send())
    for t in range(subs):
        chan_peers(lambda peer: msg_copy(t, mc, peer).wait_send())
        chan_peers(lambda peer: grd_copy(t, mc, peer).wait_send())
        chan_peers(lambda peer: upd_copy(t, mc, peer).wait_send())


def layer(n, nc, wavevectors, positions, features, filt, weight_in, weight_out, cotangent):
    atoms, channels = features.shape
    total_rows = 2 * wavevectors.shape[1]
    chunks = total_rows // (n * BLOCK)
    own = atoms // nc
    subs = own // min(BLOCK, own)
    vmem = pl.BlockSpec(memory_space=pltpu.VMEM)
    block = (chunks, n, BLOCK, channels)
    spread = pltpu.VMEM((nc, own, channels), jnp.bfloat16)
    atom_sems = pltpu.SemaphoreType.DMA((chunks, n))
    one_sem = pltpu.SemaphoreType.DMA((nc,))
    sub_sems = pltpu.SemaphoreType.DMA((subs, nc))
    return pl.pallas_call(
        functools.partial(layer_kernel, n, nc, chunks),
        out_shape=(
            jax.ShapeDtypeStruct((atoms, channels), jnp.bfloat16),
            jax.ShapeDtypeStruct((atoms, channels), jnp.float32),
        ),
        in_specs=[vmem] * 7,
        out_specs=(vmem, vmem),
        scratch_shapes=[
            pltpu.VMEM((16, wavevectors.shape[1]), jnp.bfloat16),
            pltpu.VMEM((16, atoms), jnp.bfloat16),
            pltpu.VMEM((total_rows, atoms), jnp.bfloat16),
            pltpu.VMEM(block, jnp.float32),
            pltpu.VMEM(block, jnp.bfloat16),
            pltpu.VMEM(block, jnp.bfloat16),
            pltpu.VMEM((chunks, n, channels, BLOCK), jnp.bfloat16),
            pltpu.VMEM((channels, atoms), jnp.float32),
        ] + [spread] * 7 + [atom_sems] * 4 + [one_sem] * 2 + [sub_sems] * 6,
        compiler_params=pltpu.CompilerParams(
            collective_id=0, has_side_effects=True, vmem_limit_bytes=48 * 2**20
        ),
        name="layer",
    )(wavevectors, positions, features, filt, weight_in, weight_out, cotangent)


def own_filter(wavevectors, radial_weight, atom_count, n, me):
    kvec = wavevectors.shape[1]
    waves = n * BLOCK // 2
    chunked = wavevectors.reshape(3, kvec // waves, n // 2, BLOCK)
    own = lax.dynamic_index_in_dim(chunked, lax.rem(me, n // 2), 2, keepdims=False).reshape(3, -1)
    lengths = jnp.sqrt(jnp.sum((own * own).astype(jnp.float32), 0))
    spacing = KMAX * math.sqrt(3.0) / (NB - 1)
    centers = jnp.arange(NB).astype(jnp.float32) * spacing
    basis = jnp.exp(-0.5 * ((lengths[:, None] - centers[None, :]) / spacing) ** 2)
    filt = jnp.dot(
        basis, radial_weight, precision=lax.Precision.HIGHEST, preferred_element_type=jnp.float32
    )
    return filt * (2.0 * kvec * atom_count) ** (-0.5)


def shards(features, positions, wavevectors, radial_weight, weight_in, weight_out, cotangent):
    local_atoms = features.shape[0]
    n = lax.axis_size("atoms")
    atom_count = local_atoms * n
    filt = own_filter(wavevectors, radial_weight, atom_count, n, lax.axis_index("atoms"))
    return layer(
        n, lax.axis_size("chan"), wavevectors, positions, features, filt,
        weight_in, weight_out, cotangent,
    )


def solution(mesh):
    placed = (
        P("atoms", "chan"),
        P(None, "atoms"),
        P(),
        P(None, "chan"),
        P(),
        P(),
        P("atoms", "chan"),
    )
    return jax.shard_map(
        shards,
        mesh=mesh,
        in_specs=placed,
        out_specs=(P("atoms", "chan"), P("atoms", "chan")),
        check_vma=False,
    )
```

```python
import functools
import math

import jax
import jax.numpy as jnp
import numpy as np
from jax import lax
from jax.experimental import pallas as pl
from jax.experimental.pallas import tpu as pltpu
from jax.sharding import PartitionSpec as P

NB = 16
KMAX = 8
GRID = 4096
MESH = pl.DeviceIdType.MESH
BLOCK = 128


def fit_even(fn, degree):
    cheb = np.polynomial.chebyshev.Chebyshev.interpolate(
        lambda u: fn(np.sqrt(u)), degree, domain=[0.0, 0.25]
    )
    return [float(v) for v in cheb.convert(kind=np.polynomial.Polynomial, domain=[-1, 1], window=[-1, 1]).coef]


def sin_over(f):
    return math.sqrt(2.0) * math.pi * np.sinc(f)


def cos_half(f):
    return math.sqrt(2.0) * np.cos(math.pi * f)


SIN_COEF = fit_even(sin_over, 3)
COS_COEF = fit_even(cos_half, 3)


def horner(coef, u):
    total = coef[-1] * u + coef[-2]
    for c in coef[-3::-1]:
        total = total * u + c
    return total


def layer_kernel(n, nc, chunks, *refs):
    (waves_in, place_in, x_hbm, filt_ref, w_in_hbm, w_out_hbm, cot_hbm, out_ref, grad_ref,
     x_ref, cot_ref, w_in, w_out, fetch_sem,
     wave_ref, place_ref, ph, part, pair_tx, pair_rx, hop_tx, hop_rx, ag, acc,
     cot_rx, msg_tx, msg_rx, upd_tx, upd_rx, grd_tx, grd_rx,
     pair_send, pair_recv, fwd_send, fwd_recv, hop_send, hop_recv, ag_send, ag_recv, cot_send, cot_recv,
     msg_send, msg_recv, upd_send, upd_recv, grd_send, grd_recv) = refs
    fetch = [
        pltpu.make_async_copy(src, dst, fetch_sem.at[i])
        for i, (src, dst) in enumerate(
            ((x_hbm, x_ref), (cot_hbm, cot_ref), (w_in_hbm, w_in), (w_out_hbm, w_out))
        )
    ]
    for copy in fetch:
        copy.start()
    me = lax.axis_index("atoms")
    mc = lax.axis_index("chan")
    atoms, channels = x_ref.shape
    rows = n * BLOCK
    waves = rows // 2
    own = atoms // nc
    sub = min(BLOCK, own)
    subs = own // sub
    f32, bf16 = jnp.float32, jnp.bfloat16

    def peers(fn):
        def body(step, carry):
            fn(lax.rem(me + step, n))
            return carry

        lax.fori_loop(1, n, body, 0)

    def chan_peers(fn):
        def body(step, carry):
            fn(lax.rem(mc + step, nc))
            return carry

        lax.fori_loop(1, nc, body, 0)

    barrier = pltpu.get_barrier_semaphore()
    peers(lambda peer: pl.semaphore_signal(
        barrier, inc=1, device_id={"atoms": peer}, device_id_type=MESH))
    chan_peers(lambda peer: pl.semaphore_signal(
        barrier, inc=1, device_id={"chan": peer}, device_id_type=MESH))

    half = n // 2
    chip, core = me // 2, lax.rem(me, 2)
    mine = core * half
    sibling = me + 1 - 2 * core

    def pair_copy(j):
        return pltpu.make_async_remote_copy(
            src_ref=pair_tx.at[j, pl.ds((1 - core) * half, half)],
            dst_ref=pair_rx.at[j],
            send_sem=pair_send.at[j],
            recv_sem=pair_recv.at[j],
            device_id={"atoms": sibling},
            device_id_type=MESH,
        )

    def hop_copy(j, here, there):
        return pltpu.make_async_remote_copy(
            src_ref=hop_tx.at[j, there],
            dst_ref=hop_rx.at[j, here],
            send_sem=hop_send.at[j, there],
            recv_sem=hop_recv.at[j, here],
            device_id={"atoms": 2 * there + core},
            device_id_type=MESH,
        )

    def ag_copy(j, owner, there):
        return pltpu.make_async_remote_copy(
            src_ref=ag.at[j, mine + owner],
            dst_ref=ag.at[j, mine + owner],
            send_sem=ag_send.at[j, there],
            recv_sem=ag_recv.at[j, owner],
            device_id={"atoms": 2 * there + core},
            device_id_type=MESH,
        )

    def fwd_copy(j, which):
        span = pl.ds(which * half, half)
        return pltpu.make_async_remote_copy(
            src_ref=ag.at[j, span],
            dst_ref=ag.at[j, span],
            send_sem=fwd_send.at[j],
            recv_sem=fwd_recv.at[j],
            device_id={"atoms": sibling},
            device_id_type=MESH,
        )

    def chips(fn):
        def body(step, carry):
            fn(lax.rem(chip + step, half))
            return carry

        lax.fori_loop(1, half, body, 0)

    def cot_copy(here, there):
        return pltpu.make_async_remote_copy(
            src_ref=cot_ref.at[pl.ds(pl.multiple_of(there * own, own), own)],
            dst_ref=cot_rx.at[here],
            send_sem=cot_send.at[there],
            recv_sem=cot_recv.at[here],
            device_id={"chan": there},
            device_id_type=MESH,
        )

    def sub_copy(src, dst, send, recv, t, here, there):
        span = pl.ds(t * sub, sub)
        return pltpu.make_async_remote_copy(
            src_ref=src.at[there, span],
            dst_ref=dst.at[here, span],
            send_sem=send.at[t, there],
            recv_sem=recv.at[t, here],
            device_id={"chan": there},
            device_id_type=MESH,
        )

    msg_copy = functools.partial(sub_copy, msg_tx, msg_rx, msg_send, msg_recv)
    upd_copy = functools.partial(sub_copy, upd_tx, upd_rx, upd_send, upd_recv)
    grd_copy = functools.partial(sub_copy, grd_tx, grd_rx, grd_send, grd_recv)

    k = waves_in[...].astype(f32)
    wave_ref[...] = jnp.concatenate(
        [k * (64.0 / GRID), k * (1.0 / GRID), jnp.zeros((10, k.shape[1]), f32)], 0
    ).astype(bf16)
    r = place_in[...]
    high = lax.shift_right_logical(r, 6)
    place_ref[...] = jnp.concatenate(
        [high.astype(f32), (r - high * 64).astype(f32), jnp.zeros((10, r.shape[1]), f32)], 0
    ).astype(bf16)

    tile = min(256, atoms)

    def generate(j):
        top = j * rows

        def body(a, carry):
            cols = pl.ds(pl.multiple_of(a * tile, tile), tile)
            turns = lax.dot_general(
                wave_ref[:, pl.ds(j * waves, waves)], place_ref[:, cols],
                (((0,), (0,)), ((), ())), preferred_element_type=f32,
            )
            f = turns - jnp.round(turns)
            u = f * f
            s = f * horner(SIN_COEF, u)
            c = horner(COS_COEF, u)
            ph[pl.ds(top, waves), cols] = (1.0 - s * s).astype(bf16)
            ph[pl.ds(top + waves, waves), cols] = (s * c).astype(bf16)
            return carry

        lax.fori_loop(0, atoms // tile, body, 0)

    group = min(4, n)

    def project(j, field):
        def body(i, carry):
            span = pl.ds(pl.multiple_of(j * rows + i * (group * BLOCK), group * BLOCK), group * BLOCK)
            value = jnp.dot(ph[span, :], field(), preferred_element_type=f32)
            value = value.reshape(group, BLOCK, value.shape[-1])
            slots = pl.ds(i * group, group)
            part[j, slots] = value
            pair_tx[j, slots] = value.astype(bf16)
            return carry

        lax.fori_loop(0, n // group, body, 0)

    def hop(j):
        pair_copy(j).wait_recv()

        def send(peer):
            total = part[j, mine + peer] + pair_rx[j, peer].astype(f32)
            hop_tx[j, peer] = total.astype(bf16)
            hop_copy(j, chip, peer).start()

        chips(send)

    def reduce(j):
        def body(step, total):
            peer = lax.rem(chip + step, half)
            hop_copy(j, peer, chip).wait_recv()
            return total + hop_rx[j, peer].astype(f32)

        start = part[j, mine + chip] + pair_rx[j, chip].astype(f32)
        total = lax.fori_loop(1, half, body, start)
        shaped = filt_ref[pl.ds(j * BLOCK, BLOCK), :] * total
        ag[j, mine + chip] = shaped.T.astype(bf16)
        chips(lambda peer: ag_copy(j, chip, peer).start())

    def forward(j):
        chips(lambda peer: ag_copy(j, peer, chip).wait_recv())
        fwd_copy(j, core).start()

    def back(j, emit):
        fwd_copy(j, 1 - core).wait_recv()
        lhs = jnp.concatenate([ag[j, d] for d in range(n)], axis=1)

        def body(a, carry):
            cols = pl.ds(pl.multiple_of(a * own, own), own)
            value = jnp.dot(lhs, ph[pl.ds(j * rows, rows), cols], preferred_element_type=f32)
            if j > 0:
                value = value + acc[:, cols]
            if j < chunks - 1:
                acc[:, cols] = value
            else:
                emit(a, value.T)
            return carry

        lax.fori_loop(0, nc, body, 0)

    def ewald(first, field, emit):
        for i in range(chunks + 4):
            if i < chunks:
                if first:
                    generate(i)
                if first and i == 0:
                    fetch[0].wait()
                project(i, field)
                if first and i == 0:
                    pl.semaphore_wait(barrier, n - 1 + nc - 1)
                    fetch[1].wait()
                    chan_peers(lambda peer: cot_copy(mc, peer).start())
                pair_copy(i).start()
            if 1 <= i <= chunks:
                hop(i - 1)
            if 2 <= i <= chunks + 1:
                reduce(i - 2)
            if 3 <= i <= chunks + 2:
                forward(i - 3)
            if i >= 4:
                back(i - 4, emit)
        for j in range(chunks):
            pair_copy(j).wait_send()
            chips(lambda peer: hop_copy(j, chip, peer).wait_send())
            chips(lambda peer: ag_copy(j, chip, peer).wait_send())
            fwd_copy(j, core).wait_send()

    def emit_message(a, value):
        msg_tx[a] = value.astype(bf16)

    ewald(True, lambda: x_ref[...], emit_message)

    for t in range(subs):
        chan_peers(lambda peer: msg_copy(t, mc, peer).start())
    fetch[2].wait()
    fetch[3].wait()
    msg_rx[mc] = msg_tx[mc]
    cot_rx[mc] = cot_ref[pl.ds(pl.multiple_of(mc * own, own), own), :]
    chan_peers(lambda peer: cot_copy(peer, mc).wait_recv())

    for t in range(subs):
        span = pl.ds(t * sub, sub)
        chan_peers(lambda peer: msg_copy(t, peer, mc).wait_recv())
        message = jnp.concatenate([msg_rx[c, span, :] for c in range(nc)], 1).astype(f32)
        inverse = 1.0 / jnp.sqrt(jnp.mean(message * message, -1, keepdims=True) + 1e-06)
        unit = message * inverse
        pre = jnp.dot(unit.astype(bf16), w_in[...], preferred_element_type=f32)
        gate = jax.nn.sigmoid(pre)
        update = jnp.dot((pre * gate).astype(bf16), w_out[...], preferred_element_type=f32)
        cot = jnp.concatenate([cot_rx[c, span, :] for c in range(nc)], 1)
        g_hidden = lax.dot_general(
            cot, w_out[...], (((1,), (1,)), ((), ())), preferred_element_type=f32
        )
        g_pre = (g_hidden * gate * (1.0 + pre * (1.0 - gate))).astype(bf16)
        g_normed = lax.dot_general(
            g_pre, w_in[...], (((1,), (1,)), ((), ())), preferred_element_type=f32
        )
        g_message = (
            (g_normed - unit * jnp.mean(g_normed * unit, -1, keepdims=True)) * inverse
        ).astype(bf16)
        update = update.astype(bf16)
        for c in range(nc):
            grd_tx[c, span, :] = g_message[:, c * channels:(c + 1) * channels]
            upd_tx[c, span, :] = update[:, c * channels:(c + 1) * channels]
        chan_peers(lambda peer: grd_copy(t, mc, peer).start())

    for t in range(subs):
        chan_peers(lambda peer: upd_copy(t, mc, peer).start())
    grd_rx[mc] = grd_tx[mc]
    upd_rx[mc] = upd_tx[mc]
    for t in range(subs):
        chan_peers(lambda peer: grd_copy(t, peer, mc).wait_recv())

    def emit_grad(a, value):
        span = pl.ds(pl.multiple_of(a * own, own), own)
        grad_ref[span, :] = cot_ref[span, :].astype(f32) + value

    ewald(False, lambda: grd_rx[...].reshape(atoms, channels), emit_grad)

    for t in range(subs):
        chan_peers(lambda peer: upd_copy(t, peer, mc).wait_recv())

    def add_update(c, carry):
        span = pl.ds(pl.multiple_of(c * own, own), own)
        out_ref[span, :] = (x_ref[span, :].astype(f32) + upd_rx[c].astype(f32)).astype(bf16)
        return carry

    lax.fori_loop(0, nc, add_update, 0)
    chan_peers(lambda peer: cot_copy(mc, peer).wait_send())
    for t in range(subs):
        chan_peers(lambda peer: msg_copy(t, mc, peer).wait_send())
        chan_peers(lambda peer: grd_copy(t, mc, peer).wait_send())
        chan_peers(lambda peer: upd_copy(t, mc, peer).wait_send())


def layer(n, nc, wavevectors, positions, features, filt, weight_in, weight_out, cotangent):
    atoms, channels = features.shape
    total_rows = 2 * wavevectors.shape[1]
    chunks = total_rows // (n * BLOCK)
    own = atoms // nc
    subs = own // min(BLOCK, own)
    vmem = pl.BlockSpec(memory_space=pltpu.VMEM)
    block = (chunks, n, BLOCK, channels)
    hbm = pl.BlockSpec(memory_space=pltpu.HBM)
    halved = pltpu.VMEM((chunks, n // 2, BLOCK, channels), jnp.bfloat16)
    spread = pltpu.VMEM((nc, own, channels), jnp.bfloat16)
    atom_sems = pltpu.SemaphoreType.DMA((chunks, n // 2))
    chunk_sem = pltpu.SemaphoreType.DMA((chunks,))
    one_sem = pltpu.SemaphoreType.DMA((nc,))
    sub_sems = pltpu.SemaphoreType.DMA((subs, nc))
    return pl.pallas_call(
        functools.partial(layer_kernel, n, nc, chunks),
        out_shape=(
            jax.ShapeDtypeStruct((atoms, channels), jnp.bfloat16),
            jax.ShapeDtypeStruct((atoms, channels), jnp.float32),
        ),
        in_specs=[vmem, vmem, hbm, vmem, hbm, hbm, hbm],
        out_specs=(vmem, vmem),
        scratch_shapes=[
            pltpu.VMEM(features.shape, jnp.bfloat16),
            pltpu.VMEM(cotangent.shape, jnp.bfloat16),
            pltpu.VMEM(weight_in.shape, jnp.bfloat16),
            pltpu.VMEM(weight_out.shape, jnp.bfloat16),
            pltpu.SemaphoreType.DMA((4,)),
            pltpu.VMEM((16, wavevectors.shape[1]), jnp.bfloat16),
            pltpu.VMEM((16, atoms), jnp.bfloat16),
            pltpu.VMEM((total_rows, atoms), jnp.bfloat16),
            pltpu.VMEM(block, jnp.float32),
            pltpu.VMEM(block, jnp.bfloat16),
            halved, halved, halved,
            pltpu.VMEM((chunks, n, channels, BLOCK), jnp.bfloat16),
            pltpu.VMEM((channels, atoms), jnp.float32),
        ] + [spread] * 7 + [chunk_sem] * 4 + [atom_sems] * 4 + [one_sem] * 2 + [sub_sems] * 6,
        compiler_params=pltpu.CompilerParams(
            collective_id=0, has_side_effects=True, vmem_limit_bytes=48 * 2**20
        ),
        name="layer",
    )(wavevectors, positions, features, filt, weight_in, weight_out, cotangent)


def own_filter(wavevectors, radial_weight, atom_count, n, me):
    kvec = wavevectors.shape[1]
    waves = n * BLOCK // 2
    own = jnp.concatenate([
        lax.dynamic_slice_in_dim(wavevectors, j * waves + (me // 2) * BLOCK, BLOCK, 1)
        for j in range(kvec // waves)
    ], 1)
    lengths = jnp.sqrt(jnp.sum((own * own).astype(jnp.float32), 0))
    spacing = KMAX * math.sqrt(3.0) / (NB - 1)
    centers = jnp.arange(NB).astype(jnp.float32) * spacing
    basis = jnp.exp(-0.5 * ((lengths[:, None] - centers[None, :]) / spacing) ** 2)
    filt = jnp.dot(
        basis, radial_weight, precision=lax.Precision.HIGHEST, preferred_element_type=jnp.float32
    )
    return filt * (2.0 * kvec * atom_count) ** (-0.5)


def shards(features, positions, wavevectors, radial_weight, weight_in, weight_out, cotangent):
    local_atoms = features.shape[0]
    n = lax.axis_size("atoms")
    atom_count = local_atoms * n
    filt = own_filter(wavevectors, radial_weight, atom_count, n, lax.axis_index("atoms"))
    return layer(
        n, lax.axis_size("chan"), wavevectors, positions, features, filt,
        weight_in, weight_out, cotangent,
    )


def solution(mesh):
    placed = (
        P("atoms", "chan"),
        P(None, "atoms"),
        P(),
        P(None, "chan"),
        P(),
        P(),
        P("atoms", "chan"),
    )
    return jax.shard_map(
        shards,
        mesh=mesh,
        in_specs=placed,
        out_specs=(P("atoms", "chan"), P("atoms", "chan")),
        check_vma=False,
    )
```

```python
import functools
import math

import jax
import jax.numpy as jnp
import numpy as np
from jax import lax
from jax.experimental import pallas as pl
from jax.experimental.pallas import tpu as pltpu
from jax.sharding import PartitionSpec as P

NB = 16
KMAX = 8
GRID = 4096
MESH = pl.DeviceIdType.MESH
BLOCK = 128


def fit_even(fn, degree):
    cheb = np.polynomial.chebyshev.Chebyshev.interpolate(
        lambda u: fn(np.sqrt(u)), degree, domain=[0.0, 0.25]
    )
    return [float(v) for v in cheb.convert(kind=np.polynomial.Polynomial, domain=[-1, 1], window=[-1, 1]).coef]


def sin_over(f):
    return math.sqrt(2.0) * math.pi * np.sinc(f)


def cos_half(f):
    return math.sqrt(2.0) * np.cos(math.pi * f)


SIN_COEF = fit_even(sin_over, 3)
COS_COEF = fit_even(cos_half, 3)


def horner(coef, u):
    total = coef[-1] * u + coef[-2]
    for c in coef[-3::-1]:
        total = total * u + c
    return total


def layer_kernel(n, nc, chunks, *refs):
    (waves_in, place_in, x_hbm, filt_ref, w_in_hbm, w_out_hbm, cot_hbm, out_ref, grad_ref,
     x_ref, cot_ref, w_in, w_out, fetch_sem,
     wave_ref, place_ref, ph, part, pair_tx, pair_rx, hop_tx, hop_rx, ag, acc,
     cot_rx, msg_tx, msg_rx, upd_tx, upd_rx, grd_tx, grd_rx,
     pair_send, pair_recv, fwd_send, fwd_recv, hop_send, hop_recv, ag_send, ag_recv, cot_send, cot_recv,
     msg_send, msg_recv, upd_send, upd_recv, grd_send, grd_recv) = refs
    fetch = [
        pltpu.make_async_copy(src, dst, fetch_sem.at[i])
        for i, (src, dst) in enumerate(
            ((x_hbm, x_ref), (cot_hbm, cot_ref), (w_in_hbm, w_in), (w_out_hbm, w_out))
        )
    ]
    for copy in fetch:
        copy.start()
    me = lax.axis_index("atoms")
    mc = lax.axis_index("chan")
    atoms, channels = x_ref.shape
    rows = n * BLOCK
    waves = rows // 2
    own = atoms // nc
    sub = min(BLOCK, own)
    subs = own // sub
    f32, bf16 = jnp.float32, jnp.bfloat16

    def peers(fn):
        def body(step, carry):
            fn(lax.rem(me + step, n))
            return carry

        lax.fori_loop(1, n, body, 0)

    def chan_peers(fn):
        def body(step, carry):
            fn(lax.rem(mc + step, nc))
            return carry

        lax.fori_loop(1, nc, body, 0)

    barrier = pltpu.get_barrier_semaphore()
    peers(lambda peer: pl.semaphore_signal(
        barrier, inc=1, device_id={"atoms": peer}, device_id_type=MESH))
    chan_peers(lambda peer: pl.semaphore_signal(
        barrier, inc=1, device_id={"chan": peer}, device_id_type=MESH))

    half = n // 2
    chip, core = me // 2, lax.rem(me, 2)
    mine = core * half
    sibling = me + 1 - 2 * core

    def pair_copy(j):
        return pltpu.make_async_remote_copy(
            src_ref=pair_tx.at[j, pl.ds((1 - core) * half, half)],
            dst_ref=pair_rx.at[j],
            send_sem=pair_send.at[j],
            recv_sem=pair_recv.at[j],
            device_id={"atoms": sibling},
            device_id_type=MESH,
        )

    def hop_copy(j, here, there):
        return pltpu.make_async_remote_copy(
            src_ref=hop_tx.at[j, there],
            dst_ref=hop_rx.at[j, here],
            send_sem=hop_send.at[j, there],
            recv_sem=hop_recv.at[j, here],
            device_id={"atoms": 2 * there + core},
            device_id_type=MESH,
        )

    def ag_copy(j, owner, there):
        return pltpu.make_async_remote_copy(
            src_ref=ag.at[j, mine + owner],
            dst_ref=ag.at[j, mine + owner],
            send_sem=ag_send.at[j, there],
            recv_sem=ag_recv.at[j, owner],
            device_id={"atoms": 2 * there + core},
            device_id_type=MESH,
        )

    def fwd_copy(j, which):
        span = pl.ds(which * half, half)
        return pltpu.make_async_remote_copy(
            src_ref=ag.at[j, span],
            dst_ref=ag.at[j, span],
            send_sem=fwd_send.at[j],
            recv_sem=fwd_recv.at[j],
            device_id={"atoms": sibling},
            device_id_type=MESH,
        )

    def chips(fn):
        def body(step, carry):
            fn(lax.rem(chip + step, half))
            return carry

        lax.fori_loop(1, half, body, 0)

    def cot_copy(here, there):
        return pltpu.make_async_remote_copy(
            src_ref=cot_ref.at[pl.ds(pl.multiple_of(there * own, own), own)],
            dst_ref=cot_rx.at[here],
            send_sem=cot_send.at[there],
            recv_sem=cot_recv.at[here],
            device_id={"chan": there},
            device_id_type=MESH,
        )

    def sub_copy(src, dst, send, recv, t, here, there):
        span = pl.ds(t * sub, sub)
        return pltpu.make_async_remote_copy(
            src_ref=src.at[there, span],
            dst_ref=dst.at[here, span],
            send_sem=send.at[t, there],
            recv_sem=recv.at[t, here],
            device_id={"chan": there},
            device_id_type=MESH,
        )

    msg_copy = functools.partial(sub_copy, msg_tx, msg_rx, msg_send, msg_recv)
    upd_copy = functools.partial(sub_copy, upd_tx, upd_rx, upd_send, upd_recv)
    grd_copy = functools.partial(sub_copy, grd_tx, grd_rx, grd_send, grd_recv)

    k = waves_in[...].astype(f32)
    wave_ref[...] = jnp.concatenate(
        [k * (64.0 / GRID), k * (1.0 / GRID), jnp.zeros((10, k.shape[1]), f32)], 0
    ).astype(bf16)
    r = place_in[...]
    high = lax.shift_right_logical(r, 6)
    place_ref[...] = jnp.concatenate(
        [high.astype(f32), (r - high * 64).astype(f32), jnp.zeros((10, r.shape[1]), f32)], 0
    ).astype(bf16)

    tile = min(256, atoms)

    def generate(j):
        top = j * rows

        def body(a, carry):
            cols = pl.ds(pl.multiple_of(a * tile, tile), tile)
            turns = lax.dot_general(
                wave_ref[:, pl.ds(j * waves, waves)], place_ref[:, cols],
                (((0,), (0,)), ((), ())), preferred_element_type=f32,
            )
            f = turns - jnp.round(turns)
            u = f * f
            s = f * horner(SIN_COEF, u)
            c = horner(COS_COEF, u)
            ph[pl.ds(top, waves), cols] = (1.0 - s * s).astype(bf16)
            ph[pl.ds(top + waves, waves), cols] = (s * c).astype(bf16)
            return carry

        lax.fori_loop(0, atoms // tile, body, 0)

    group = min(4, n)

    def project(j, field):
        def body(i, carry):
            span = pl.ds(pl.multiple_of(j * rows + i * (group * BLOCK), group * BLOCK), group * BLOCK)
            value = jnp.dot(ph[span, :], field(), preferred_element_type=f32)
            value = value.reshape(group, BLOCK, value.shape[-1])
            slots = pl.ds(i * group, group)
            part[j, slots] = value
            pair_tx[j, slots] = value.astype(bf16)
            return carry

        lax.fori_loop(0, n // group, body, 0)

    def hop(j):
        pair_copy(j).wait_recv()

        def send(peer):
            total = part[j, mine + peer] + pair_rx[j, peer].astype(f32)
            hop_tx[j, peer] = total.astype(bf16)
            hop_copy(j, chip, peer).start()

        chips(send)

    def reduce(j):
        def body(step, total):
            peer = lax.rem(chip + step, half)
            hop_copy(j, peer, chip).wait_recv()
            return total + hop_rx[j, peer].astype(f32)

        start = part[j, mine + chip] + pair_rx[j, chip].astype(f32)
        total = lax.fori_loop(1, half, body, start)
        shaped = filt_ref[pl.ds(j * BLOCK, BLOCK), :] * total
        ag[j, mine + chip] = shaped.T.astype(bf16)
        chips(lambda peer: ag_copy(j, chip, peer).start())

    def forward(j):
        chips(lambda peer: ag_copy(j, peer, chip).wait_recv())
        fwd_copy(j, core).start()

    def back(j, emit):
        fwd_copy(j, 1 - core).wait_recv()
        lhs = jnp.concatenate([ag[j, d] for d in range(n)], axis=1)

        def body(a, carry):
            cols = pl.ds(pl.multiple_of(a * own, own), own)
            value = jnp.dot(lhs, ph[pl.ds(j * rows, rows), cols], preferred_element_type=f32)
            if j > 0:
                value = value + acc[:, cols]
            if j < chunks - 1:
                acc[:, cols] = value
            else:
                emit(a, value.T)
            return carry

        lax.fori_loop(0, nc, body, 0)

    def ewald(first, field, emit):
        for i in range(chunks + 4):
            if i < chunks:
                if first:
                    generate(i)
                if first and i == 0:
                    fetch[0].wait()
                project(i, field)
                if first and i == 0:
                    pl.semaphore_wait(barrier, n - 1 + nc - 1)
                    fetch[1].wait()
                    chan_peers(lambda peer: cot_copy(mc, peer).start())
                pair_copy(i).start()
            if 1 <= i <= chunks:
                hop(i - 1)
            if 2 <= i <= chunks + 1:
                reduce(i - 2)
            if 3 <= i <= chunks + 2:
                forward(i - 3)
            if i >= 4:
                back(i - 4, emit)
        for j in range(chunks):
            pair_copy(j).wait_send()
            chips(lambda peer: hop_copy(j, chip, peer).wait_send())
            chips(lambda peer: ag_copy(j, chip, peer).wait_send())
            fwd_copy(j, core).wait_send()

    def emit_message(a, value):
        msg_tx[a] = value.astype(bf16)

    ewald(True, lambda: x_ref[...], emit_message)

    for t in range(subs):
        chan_peers(lambda peer: msg_copy(t, mc, peer).start())
    fetch[2].wait()
    fetch[3].wait()
    msg_rx[mc] = msg_tx[mc]
    cot_rx[mc] = cot_ref[pl.ds(pl.multiple_of(mc * own, own), own), :]
    chan_peers(lambda peer: cot_copy(peer, mc).wait_recv())

    for t in range(subs):
        span = pl.ds(t * sub, sub)
        chan_peers(lambda peer: msg_copy(t, peer, mc).wait_recv())
        message = jnp.concatenate([msg_rx[c, span, :] for c in range(nc)], 1).astype(f32)
        inverse = 1.0 / jnp.sqrt(jnp.mean(message * message, -1, keepdims=True) + 1e-06)
        unit = message * inverse
        pre = jnp.dot(unit.astype(bf16), w_in[...], preferred_element_type=f32)
        gate = jax.nn.sigmoid(pre)
        update = jnp.dot((pre * gate).astype(bf16), w_out[...], preferred_element_type=f32)
        cot = jnp.concatenate([cot_rx[c, span, :] for c in range(nc)], 1)
        g_hidden = lax.dot_general(
            cot, w_out[...], (((1,), (1,)), ((), ())), preferred_element_type=f32
        )
        g_pre = (g_hidden * gate * (1.0 + pre * (1.0 - gate))).astype(bf16)
        g_normed = lax.dot_general(
            g_pre, w_in[...], (((1,), (1,)), ((), ())), preferred_element_type=f32
        )
        g_message = (
            (g_normed - unit * jnp.mean(g_normed * unit, -1, keepdims=True)) * inverse
        ).astype(bf16)
        update = update.astype(bf16)
        for c in range(nc):
            grd_tx[c, span, :] = g_message[:, c * channels:(c + 1) * channels]
            upd_tx[c, span, :] = update[:, c * channels:(c + 1) * channels]
        chan_peers(lambda peer: grd_copy(t, mc, peer).start())

    for t in range(subs):
        chan_peers(lambda peer: upd_copy(t, mc, peer).start())
    grd_rx[mc] = grd_tx[mc]
    upd_rx[mc] = upd_tx[mc]
    for t in range(subs):
        chan_peers(lambda peer: grd_copy(t, peer, mc).wait_recv())

    def emit_grad(a, value):
        span = pl.ds(pl.multiple_of(a * own, own), own)
        grad_ref[span, :] = cot_ref[span, :].astype(f32) + value

    ewald(False, lambda: grd_rx[...].reshape(atoms, channels), emit_grad)

    for t in range(subs):
        chan_peers(lambda peer: upd_copy(t, peer, mc).wait_recv())

    def add_update(c, carry):
        span = pl.ds(pl.multiple_of(c * own, own), own)
        out_ref[span, :] = (x_ref[span, :].astype(f32) + upd_rx[c].astype(f32)).astype(bf16)
        return carry

    lax.fori_loop(0, nc, add_update, 0)
    chan_peers(lambda peer: cot_copy(mc, peer).wait_send())
    for t in range(subs):
        chan_peers(lambda peer: msg_copy(t, mc, peer).wait_send())
        chan_peers(lambda peer: grd_copy(t, mc, peer).wait_send())
        chan_peers(lambda peer: upd_copy(t, mc, peer).wait_send())


def layer(n, nc, wavevectors, positions, features, filt, weight_in, weight_out, cotangent):
    atoms, channels = features.shape
    total_rows = 2 * wavevectors.shape[1]
    chunks = total_rows // (n * BLOCK)
    own = atoms // nc
    subs = own // min(BLOCK, own)
    vmem = pl.BlockSpec(memory_space=pltpu.VMEM)
    block = (chunks, n, BLOCK, channels)
    hbm = pl.BlockSpec(memory_space=pltpu.HBM)
    halved = pltpu.VMEM((chunks, n // 2, BLOCK, channels), jnp.bfloat16)
    spread = pltpu.VMEM((nc, own, channels), jnp.bfloat16)
    atom_sems = pltpu.SemaphoreType.DMA((chunks, n // 2))
    chunk_sem = pltpu.SemaphoreType.DMA((chunks,))
    one_sem = pltpu.SemaphoreType.DMA((nc,))
    sub_sems = pltpu.SemaphoreType.DMA((subs, nc))
    return pl.pallas_call(
        functools.partial(layer_kernel, n, nc, chunks),
        out_shape=(
            jax.ShapeDtypeStruct((atoms, channels), jnp.bfloat16),
            jax.ShapeDtypeStruct((atoms, channels), jnp.float32),
        ),
        in_specs=[vmem, vmem, hbm, vmem, hbm, hbm, hbm],
        out_specs=(vmem, vmem),
        scratch_shapes=[
            pltpu.VMEM(features.shape, jnp.bfloat16),
            pltpu.VMEM(cotangent.shape, jnp.bfloat16),
            pltpu.VMEM(weight_in.shape, jnp.bfloat16),
            pltpu.VMEM(weight_out.shape, jnp.bfloat16),
            pltpu.SemaphoreType.DMA((4,)),
            pltpu.VMEM((16, wavevectors.shape[1]), jnp.bfloat16),
            pltpu.VMEM((16, atoms), jnp.bfloat16),
            pltpu.VMEM((total_rows, atoms), jnp.bfloat16),
            pltpu.VMEM(block, jnp.float32),
            pltpu.VMEM(block, jnp.bfloat16),
            halved, halved, halved,
            pltpu.VMEM((chunks, n, channels, BLOCK), jnp.bfloat16),
            pltpu.VMEM((channels, atoms), jnp.float32),
        ] + [spread] * 7 + [chunk_sem] * 4 + [atom_sems] * 4 + [one_sem] * 2 + [sub_sems] * 6,
        compiler_params=pltpu.CompilerParams(
            collective_id=0, has_side_effects=True, vmem_limit_bytes=61 * 2**20
        ),
        name="layer",
    )(wavevectors, positions, features, filt, weight_in, weight_out, cotangent)


def own_filter(wavevectors, radial_weight, atom_count, n, me):
    kvec = wavevectors.shape[1]
    waves = n * BLOCK // 2
    own = jnp.concatenate([
        lax.dynamic_slice_in_dim(wavevectors, j * waves + (me // 2) * BLOCK, BLOCK, 1)
        for j in range(kvec // waves)
    ], 1)
    lengths = jnp.sqrt(jnp.sum((own * own).astype(jnp.float32), 0))
    spacing = KMAX * math.sqrt(3.0) / (NB - 1)
    centers = jnp.arange(NB).astype(jnp.float32) * spacing
    basis = jnp.exp(-0.5 * ((lengths[:, None] - centers[None, :]) / spacing) ** 2)
    filt = jnp.dot(
        basis, radial_weight, precision=lax.Precision.HIGHEST, preferred_element_type=jnp.float32
    )
    return filt * (2.0 * kvec * atom_count) ** (-0.5)


def shards(features, positions, wavevectors, radial_weight, weight_in, weight_out, cotangent):
    local_atoms = features.shape[0]
    n = lax.axis_size("atoms")
    atom_count = local_atoms * n
    filt = own_filter(wavevectors, radial_weight, atom_count, n, lax.axis_index("atoms"))
    return layer(
        n, lax.axis_size("chan"), wavevectors, positions, features, filt,
        weight_in, weight_out, cotangent,
    )


def solution(mesh):
    placed = (
        P("atoms", "chan"),
        P(None, "atoms"),
        P(),
        P(None, "chan"),
        P(),
        P(),
        P("atoms", "chan"),
    )
    return jax.shard_map(
        shards,
        mesh=mesh,
        in_specs=placed,
        out_specs=(P("atoms", "chan"), P("atoms", "chan")),
        check_vma=False,
    )
```
